32 devices in a mesh: head: 4 (over z), vocab: 8 (over y, x, core).
Axes of the slice: x: 2, y: 2, z: 4, core: 2. Of those that a mesh axis runs over, the one named last changes fastest.
Arguments:
- hidden_states: bfloat16 [256, 8192], P(('head', 'vocab')), may hold values from -6 to 6
- head_weight: bfloat16 [4, 8192, 16384], P('head', None, 'vocab'), may hold values from -1 to 1
- tags: int32 [256, 1], P(('head', 'vocab')), may hold values from 0 to 3; in each aligned block of 8 rows (0 to 7, 8 to 15, ...) at most 2 rows name the same one
- targets: int32 [256], P(('head', 'vocab')), may hold values from 0 to 16383
- row_grad: bfloat16 [256], P(('head', 'vocab')), may hold values from -192 to 192
Outputs:
- row_loss: bfloat16 [256], P(('head', 'vocab'))
- hidden_grad: bfloat16 [256, 8192], P(('head', 'vocab'))
The draws below stay inside these ranges and needn't reach their ends.
Inputs may be any that keep to these rules, and one draw needn't show every extreme that they name: `tags`: in each aligned block of 8 rows (the rows of one device) no head is named by more than 2 rows, and in every draw some block has exactly 2 rows of one head.
All inputs are finite; a program needn't handle non-finite values.
Results may differ from the reference program's by a relative error of at most 0.018.
Values may be sent and summed in bfloat16 or wider, within the bound.
A program may use at most 64 MiB of HBM per device.

```python
import math
import jax
import jax.numpy as jnp
import numpy as np
from jax import lax

D = 8192
VOCAB = 16384
ROW_DEV = 8
CAP = 2
HEADS = 4
ROWS = 256
N_VOCAB = 8


def base_hidden(key):
    return jnp.clip(jax.random.normal(jax.random.fold_in(key, 71), (ROWS, D), jnp.float32), -6.0, 6.0)


def draw_hidden_states(key, part):
    values = base_hidden(key)
    return values.astype(jnp.bfloat16)


def draw_head_weight(key, part):
    values = jnp.clip(jax.random.normal(jax.random.fold_in(key, 73), (HEADS, D, VOCAB), jnp.float32), -6.0, 6.0) * D ** (-0.5)
    return values.astype(jnp.bfloat16)


def place_ends(result, stream_key, smallest, top_value):
    place = [jax.random.randint(jax.random.fold_in(stream_key, axis), (), 0, length) for axis, length in enumerate(result.shape)]
    main_axis = result.shape.index(max(result.shape))
    neighbour = place[:main_axis] + [(place[main_axis] + 1) % result.shape[main_axis]] + place[main_axis + 1:]
    return result.at[tuple(place)].set(smallest).at[tuple(neighbour)].set(top_value)


def block_scale(key, shape, split, low, high):
    def one(axis_at, blocks):
        heights = jax.random.uniform(jax.random.fold_in(jax.random.fold_in(key, 6), axis_at), (blocks,), jnp.float32, low / len(split), high / len(split))
        return jnp.repeat(jnp.exp(heights), shape[axis_at] // blocks).reshape((-1,) + (1,) * (len(shape) - axis_at - 1))

    level = one(*split[0])
    for cut in split[1:]:
        level = level * one(*cut)
    return level


def shared_out(key, own, number, rows, count, top, most, lean):
    sequence = jax.random.permutation(key, count)
    crowded, usual = load_shares(count, rows * top, most, lean, True), load_shares(count, rows * top, most, lean, False)
    places = jnp.arange(count)

    def named(tallies, offset_by):
        used = int((tallies > 0).sum())
        fixed = max(1, used // 4)
        moved = fixed + (places - fixed + offset_by * (used - fixed)) % max(1, count - fixed)
        return jnp.zeros((count,), jnp.int32).at[sequence[jnp.where(places < fixed, places, moved)]].set(jnp.asarray(tallies, jnp.int32))

    tallies = jnp.where(number % 4 == 0, named(crowded, number // 4), named(usual, number - number // 4 - 1))
    mixed = jax.random.permutation(jax.random.fold_in(own, 3), count)
    donor, sink = mixed[0:count // 2 * 2:2], mixed[1:count // 2 * 2:2]
    room = jnp.minimum(tallies[donor] - 1, most - tallies[sink]) // 2
    room = jnp.where((donor == sequence[0]) | (sink == sequence[0]) | (tallies[sink] == 0), 0, jnp.maximum(room, 0))
    moved = jax.random.randint(jax.random.fold_in(own, 4), (count // 2,), 0, 1 << 20) % (room + 1)
    tallies = tallies.at[donor].add(-moved).at[sink].add(moved)
    members = jnp.searchsorted(jnp.cumsum(tallies), jnp.arange(rows * top), side="right").astype(jnp.int32)
    grid = members.reshape(top, rows).T
    grid = grid[jax.random.permutation(jax.random.fold_in(own, 1), rows)]
    offset_by = jax.random.randint(jax.random.fold_in(own, 2), (rows, 1), 0, top)
    return jnp.take_along_axis(grid, (jnp.arange(top)[None, :] + offset_by) % top, axis=1)


def load_shares(amount, total, limit, slope, full):
    portions = [(1 << 20) // math.isqrt(grade ** slope) + 1 for grade in range(1, amount + 1)]
    largest = limit if full else min(limit, max(-(-total // amount), total * portions[0] // sum(portions)))
    least = 1 if total - largest >= amount - 1 else 0
    given, surplus = [largest] + [least] * (amount - 1), total - largest - least * (amount - 1)
    while surplus > 0:
        free = [i for i in range(1, amount) if given[i] < largest] or [i for i in range(1, amount) if given[i] < limit]
        whole, remaining = sum([portions[i] for i in free]), surplus
        for i in free:
            extra = min(limit - given[i], max(1, remaining * portions[i] // whole), surplus)
            given[i] = given[i] + extra
            surplus = surplus - extra
    return np.array(given)


def normal_values(key, extent, scale, reach, shards=(), held_as=jnp.bfloat16):
    entries = scale * jax.random.normal(key, extent, jnp.float32)
    if shards:
        entries = entries * block_scale(key, extent, shards, -0.22, 0.18)
    return jnp.clip(entries, -reach, reach).astype(held_as)


def setup_inputs(seed: int = 0) -> dict:
    seeds = jax.random.split(jax.random.key(seed), 6)
    hidden_states = draw_hidden_states(jax.random.fold_in(seeds[5], 71), 0)
    head_weight = draw_head_weight(jax.random.fold_in(seeds[5], 71), 0)
    tags_keys = jax.random.split(jax.random.fold_in(seeds[2], 1), ROWS // ROW_DEV)
    tags_turns = jax.random.permutation(jax.random.fold_in(seeds[2], 3), ROWS // ROW_DEV)
    tags = jax.vmap(lambda own, number: shared_out(jax.random.fold_in(seeds[2], 2), own, number, ROW_DEV, HEADS, 1, CAP, 2))(tags_keys, tags_turns).reshape((ROWS, 1))
    targets = place_ends(jax.random.randint(seeds[3], (ROWS,), 0, VOCAB), jax.random.fold_in(seeds[3], 1), 0, VOCAB - 1).astype(jnp.int32)
    row_grad = normal_values(seeds[4], (ROWS,), 32.0, 192.0, ((0, 32),))
    return dict(hidden_states=hidden_states, head_weight=head_weight, tags=tags, targets=targets, row_grad=row_grad)


block_rows = 64


def reference(hidden_states, head_weight, tags, targets, row_grad):
    row_tag = tags[:, 0].astype(jnp.int32)
    row_order = jnp.argsort(row_tag, stable=True).astype(jnp.int32)
    head_ids = jnp.arange(HEADS, dtype=jnp.int32)
    counts = jnp.sum((row_tag[:, None] == head_ids[None, :]).astype(jnp.int32), axis=0).astype(jnp.int32)
    starts = (jnp.cumsum(counts) - counts).astype(jnp.int32)
    sorted_rows = jnp.concatenate([hidden_states[row_order], jnp.zeros((block_rows, D), hidden_states.dtype)], 0)
    sorted_targets = jnp.concatenate([targets[row_order].astype(jnp.int32), jnp.zeros((block_rows,), jnp.int32)], 0)
    sorted_scale = jnp.concatenate([row_grad[row_order].astype(jnp.float32), jnp.zeros((block_rows,), jnp.float32)], 0)
    loss_sorted = jnp.zeros((ROWS + block_rows,), jnp.float32)
    grad_sorted = jnp.zeros((ROWS + block_rows, D), jnp.bfloat16)
    position = jnp.arange(block_rows, dtype=jnp.int32)
    columns = jnp.arange(VOCAB, dtype=jnp.int32)
    for head in range(HEADS):
        weight = head_weight[head]
        weight_wide = weight.astype(jnp.float32).reshape(D, N_VOCAB, VOCAB // N_VOCAB)
        first_row = starts[head]
        last_row = (starts[head] + counts[head]).astype(jnp.int32)
        block_count = ((counts[head] + block_rows - 1) // block_rows).astype(jnp.int32)

        def block_step(index, carry, weight=weight, weight_wide=weight_wide, first_row=first_row, last_row=last_row):
            loss_now, grad_now = carry
            begin = (first_row + index * block_rows).astype(jnp.int32)
            rows_block = lax.dynamic_slice(sorted_rows, (begin, jnp.int32(0)), (block_rows, D))
            target_block = lax.dynamic_slice(sorted_targets, (begin,), (block_rows,))
            scale_block = lax.dynamic_slice(sorted_scale, (begin,), (block_rows,))
            logits = jnp.dot(rows_block, weight, preferred_element_type=jnp.float32)
            row_top = jnp.max(logits, axis=1)
            shifted = jnp.exp(logits - row_top[:, None])
            row_total = jnp.sum(shifted, axis=1)
            target_hit = columns[None, :] == target_block[:, None]
            target_logit = jnp.sum(jnp.where(target_hit, logits, 0.0), axis=1)
            loss_block = (jnp.log(row_total) + row_top - target_logit).astype(jnp.bfloat16)
            probabilities = shifted / row_total[:, None]
            dlogits = (scale_block[:, None] * (probabilities - target_hit.astype(jnp.float32))).astype(jnp.bfloat16)
            partials = jnp.einsum('rvk,dvk->vrd', dlogits.astype(jnp.float32).reshape(block_rows, N_VOCAB, VOCAB // N_VOCAB), weight_wide)
            rounded = lax.optimization_barrier(partials.astype(jnp.bfloat16))
            grad_block = jnp.sum(rounded.astype(jnp.float32), axis=0).astype(jnp.bfloat16)
            live_rows = (begin + position) < last_row
            old_loss = lax.dynamic_slice(loss_now, (begin,), (block_rows,))
            new_loss = jnp.where(live_rows, loss_block.astype(jnp.float32), old_loss)
            loss_now = lax.dynamic_update_slice(loss_now, new_loss, (begin,))
            old_grad = lax.dynamic_slice(grad_now, (begin, jnp.int32(0)), (block_rows, D))
            new_grad = jnp.where(live_rows[:, None], grad_block, old_grad)
            grad_now = lax.dynamic_update_slice(grad_now, new_grad, (begin, jnp.int32(0)))
            return (loss_now, grad_now)

        loss_sorted, grad_sorted = lax.fori_loop(jnp.int32(0), block_count, block_step, (loss_sorted, grad_sorted))
    row_loss = jnp.zeros((ROWS,), jnp.float32).at[row_order].set(loss_sorted[:ROWS]).astype(jnp.bfloat16)
    hidden_grad = jnp.zeros((ROWS, D), jnp.bfloat16).at[row_order].set(grad_sorted[:ROWS])
    return (row_loss, hidden_grad)
```

```python
import functools

import jax
import jax.numpy as jnp
from jax import lax
from jax.experimental import pallas as pl
from jax.experimental.pallas import tpu as pltpu
from jax.sharding import PartitionSpec as P

CAP = 2
CHUNKS = 8
MESH = pl.DeviceIdType.MESH
F32 = jnp.float32
BF16 = jnp.bfloat16


def iota(shape, dim):
    return lax.broadcasted_iota(jnp.int32, shape, dim).astype(F32)


def transposed(vector, axis):
    n = max(vector.shape)
    eye = iota((n, n), 0) == iota((n, n), 1)
    return jnp.sum(jnp.where(eye, vector, 0.0), axis=axis, keepdims=True)


def kernel(
    n_head, n_vocab, chunks,
    meta_ref, hidden_ref, w_hbm, loss_ref, grad_ref,
    w_ref, row_out, row_in, rows, meta_out, meta_in, meta_all, logit_ref, dlog_ref,
    stat_all, part, pair_out, pair_in, sum_out, sum_in, back_out, back_in, loss_out, loss_in,
    w_sem, row_s, row_r, meta_s, meta_r, spread_s, spread_r, share_s, share_r,
    all_s, all_r, stat_s, stat_r, pair_s, pair_r, sum_s, sum_r, back_s, back_r, loss_s, loss_r,
):
    my_head, my_vocab = lax.axis_index("head"), lax.axis_index("vocab")
    n_chip = n_vocab // 2
    chip, core = my_vocab // 2, my_vocab % 2
    own = n_head * CAP
    local, depth = hidden_ref.shape
    width = depth // chunks
    group = n_vocab * own
    columns = w_ref.shape[1]

    def span(k):
        return pl.ds(pl.multiple_of(k * width, width), width)

    def load_weight(k):
        part_k = pl.ds(pl.multiple_of(k * width, width), width)
        return pltpu.make_async_copy(w_hbm.at[0, part_k], w_ref.at[part_k], w_sem.at[k])

    for k in range(chunks):
        load_weight(k).start()

    def head_peer(d):
        return ((my_head + d) % n_head, my_vocab)

    def vocab_peer(d):
        return (my_head, (my_vocab + d) % n_vocab)

    def chip_peer(d):
        return (my_head, ((chip + d) % n_chip) * 2 + core)

    def place(v):
        return (v % 2) * n_chip + v // 2

    partner = (my_head, chip * 2 + 1 - core)
    my_place = place(my_vocab)

    def remote(src, dst, send, recv, device):
        return pltpu.make_async_remote_copy(
            src_ref=src, dst_ref=dst, send_sem=send, recv_sem=recv,
            device_id=device, device_id_type=MESH,
        )

    def send_row(d, k):
        return remote(row_out.at[d, :, span(k)], row_in.at[d, :, span(k)],
                      row_s.at[d, k], row_r.at[d, k], head_peer(d))

    def send_meta(d):
        return remote(meta_out.at[d], meta_in.at[d], meta_s.at[d], meta_r.at[d], head_peer(d))

    def spread(d, k, slot):
        return remote(rows.at[slot, :, span(k)], rows.at[slot, :, span(k)],
                      spread_s.at[d, k], spread_r.at[d, k], chip_peer(d))

    def share(d, k, slot):
        return remote(rows.at[slot, :, span(k)], rows.at[slot, :, span(k)],
                      share_s.at[d, k], share_r.at[d, k], partner)

    def send_all(d, slot):
        return remote(meta_all.at[slot], meta_all.at[slot], all_s.at[d], all_r.at[d], vocab_peer(d))

    def send_stat(d, slot):
        return remote(stat_all.at[slot], stat_all.at[slot], stat_s.at[d], stat_r.at[d], vocab_peer(d))

    def send_pair(k):
        return remote(pair_out.at[:, :, span(k)], pair_in.at[:, :, span(k)],
                      pair_s.at[k], pair_r.at[k], partner)

    def send_sum(d, k):
        return remote(sum_out.at[d, :, span(k)], sum_in.at[d, :, span(k)],
                      sum_s.at[d, k], sum_r.at[d, k], chip_peer(d))

    def send_back(d, k):
        return remote(back_out.at[d, :, span(k)], back_in.at[d, :, span(k)],
                      back_s.at[d, k], back_r.at[d, k], head_peer(d))

    def send_loss(d):
        return remote(loss_out, loss_in.at[d], loss_s.at[d], loss_r.at[d], head_peer(d))

    barrier = pltpu.get_barrier_semaphore()
    for d in range(1, n_head):
        pl.semaphore_signal(barrier, inc=1, device_id=head_peer(d), device_id_type=MESH)
    for d in range(1, n_vocab):
        pl.semaphore_signal(barrier, inc=1, device_id=vocab_peer(d), device_id_type=MESH)

    tag_row = meta_ref[0:1, :]
    target_row = meta_ref[1:2, :]
    scale_row = meta_ref[2:3, :]
    tag_col = transposed(tag_row, 1)
    earlier = (tag_col == tag_row) & (iota((local, local), 0) < iota((local, local), 1))
    rank_row = jnp.sum(jnp.where(earlier, 1.0, 0.0), axis=0, keepdims=True)
    slot_row = tag_row * CAP + rank_row
    slot_col = transposed(slot_row, 1)
    home = my_head.astype(F32)

    def head_at(d):
        return ((my_head + d + n_head) % n_head).astype(F32)

    lane = iota((own, 128), 1)
    meta_tiles = []
    for d in range(n_head):
        seat = iota((own, local), 0) - home * CAP
        mask = (slot_row == head_at(d) * CAP + seat) & (seat >= 0) & (seat < CAP)
        goal = jnp.sum(jnp.where(mask, target_row, 0.0), axis=1, keepdims=True)
        scale = jnp.sum(jnp.where(mask, scale_row, 0.0), axis=1, keepdims=True)
        tile = jnp.where(lane == 0, goal, jnp.where(lane == 1, scale, 0.0))
        (meta_in if d == 0 else meta_out)[d] = tile
    for d in range(n_head):
        chosen = jnp.where(slot_row == head_at(d) * CAP + iota((CAP, local), 0), 1.0, 0.0)
        picked = jnp.dot(chosen.astype(BF16), hidden_ref[...], preferred_element_type=F32)
        (row_in if d == 0 else row_out)[d] = picked.astype(BF16)

    pl.semaphore_wait(barrier, n_head + n_vocab - 2)

    for d in range(1, n_head):
        send_meta(d).start()

    def start_rows(k, carry):
        for d in range(1, n_head):
            send_row(d, k).start()
        return carry

    lax.fori_loop(0, chunks, start_rows, 0)

    def gather_rows(k, carry):
        total = jnp.zeros((own, width), F32)
        for d in range(n_head):
            if d:
                send_row(d, k).wait_recv()
            put = jnp.where(
                iota((own, CAP), 0) == head_at(-d) * CAP + iota((own, CAP), 1), 1.0, 0.0
            )
            total += jnp.dot(put.astype(BF16), row_in[d, :, span(k)], preferred_element_type=F32)
        rows[my_place, :, span(k)] = total.astype(BF16)
        for d in range(1, n_chip):
            spread(d, k, my_place).start()
        share(0, k, my_place).start()
        return carry

    lax.fori_loop(0, chunks, gather_rows, 0)

    tile = meta_in[0]
    for d in range(1, n_head):
        send_meta(d).wait_recv()
        tile += meta_in[d]
    meta_all[my_place] = tile
    for d in range(1, n_vocab):
        send_all(d, my_place).start()

    logit_ref[...] = jnp.zeros_like(logit_ref)

    def forward_share(k):
        for d in range(1, n_chip):
            slot = core * n_chip + (chip - d + n_chip) % n_chip
            spread(d, k, slot).wait_recv()
            share(d, k, slot).start()

    forward_share(0)

    def multiply(k, carry):
        @pl.when(k + 1 < chunks)
        def _():
            forward_share(k + 1)

        for d in range(n_chip):
            slot = (1 - core) * n_chip + (chip - d + n_chip) % n_chip
            share(d, k, slot).wait_recv()
        load_weight(k).wait()
        x = rows[:, :, span(k)].reshape(group, width)
        logit_ref[...] += jnp.dot(x, w_ref[span(k), :], preferred_element_type=F32)
        return carry

    lax.fori_loop(0, chunks, multiply, 0)

    for d in range(1, n_vocab):
        send_all(d, place((my_vocab - d + n_vocab) % n_vocab)).wait_recv()
    info = meta_all[...].reshape(group, 128)
    goal_col = info[:, 0:1] - (my_vocab * columns).astype(F32)
    scale_col = info[:, 1:2]
    logits = logit_ref[...]
    hit = iota((group, columns), 1) == goal_col
    top_col = jnp.max(logits, axis=1, keepdims=True)
    target_col = jnp.sum(jnp.where(hit, logits, 0.0), axis=1, keepdims=True)
    grown = jnp.exp(logits - top_col)
    logit_ref[...] = grown
    total_col = jnp.sum(grown, axis=1, keepdims=True)
    line = iota((8, group), 0)
    stat_all[my_place] = jnp.where(
        line == 0, transposed(top_col, 0),
        jnp.where(line == 1, transposed(total_col, 0), transposed(target_col, 0)),
    )
    for d in range(1, n_vocab):
        send_stat(d, my_place).start()
    for d in range(1, n_vocab):
        send_stat(d, place((my_vocab - d + n_vocab) % n_vocab)).wait_recv()
    tops = stat_all[:, 0, :]
    row_top = jnp.max(tops, axis=0, keepdims=True)
    row_total = jnp.sum(stat_all[:, 1, :] * jnp.exp(tops - row_top), axis=0, keepdims=True)
    row_target = jnp.sum(stat_all[:, 2, :], axis=0, keepdims=True)
    loss_row = jnp.log(row_total) + row_top - row_target
    mine = iota((own, group), 1) == iota((own, group), 0) + (my_place * own).astype(F32)
    loss_col = jnp.sum(jnp.where(mine, loss_row, 0.0), axis=1, keepdims=True)
    loss_out[...] = jnp.broadcast_to(loss_col, (own, 128))
    for d in range(1, n_head):
        send_loss(d).start()
    factor_col = scale_col * jnp.exp(top_col - transposed(row_top, 1)) / transposed(row_total, 1)
    hit = iota((group, columns), 1) == goal_col
    dlog_ref[...] = (logit_ref[...] * factor_col - jnp.where(hit, scale_col, 0.0)).astype(BF16)

    def back(k, carry):
        @pl.when(k < chunks)
        def _():
            value = lax.dot_general(
                dlog_ref[...], w_ref[span(k), :], (((1,), (1,)), ((), ())),
                preferred_element_type=F32,
            )
            part[k % 2] = value.reshape(2, n_chip, own, width)
            pair_out[:, :, span(k)] = part[k % 2, 1 - core].astype(BF16)
            send_pair(k).start()

        @pl.when((k >= 1) & (k < chunks + 1))
        def _():
            j = k - 1
            send_pair(j).wait_recv()
            for d in range(1, n_chip):
                to = (chip + d) % n_chip
                both = part[j % 2, core, to] + pair_in[to, :, span(j)].astype(F32)
                sum_out[d, :, span(j)] = both.astype(BF16)
                send_sum(d, j).start()
            both = part[j % 2, core, chip] + pair_in[chip, :, span(j)].astype(F32)
            sum_in[0, :, span(j)] = both.astype(BF16)

        @pl.when(k >= 2)
        def _():
            j = k - 2
            total = sum_in[0, :, span(j)].astype(F32)
            for d in range(1, n_chip):
                send_sum(d, j).wait_recv()
                total += sum_in[d, :, span(j)].astype(F32)
            total = total.astype(BF16)
            for d in range(n_head):
                take = jnp.where(
                    iota((CAP, own), 1) == head_at(d) * CAP + iota((CAP, own), 0), 1.0, 0.0
                )
                piece = jnp.dot(take.astype(BF16), total, preferred_element_type=F32)
                (back_out if d else back_in)[d, :, span(j)] = piece.astype(BF16)
                if d:
                    send_back(d, j).start()

        return carry

    lax.fori_loop(0, chunks + 2, back, 0)

    loss = jnp.zeros((1, local), F32)
    for d in range(n_head):
        if d:
            send_loss(d).wait_recv()
            tile = loss_in[d]
        else:
            tile = loss_out[...]
        mask = (tag_row == head_at(-d)) & (iota((own, local), 0) == home * CAP + rank_row)
        loss += jnp.sum(jnp.where(mask, tile[:, :local], 0.0), axis=0, keepdims=True)
    loss_ref[...] = loss

    def finish(k, carry):
        total = jnp.zeros((local, width), F32)
        for d in range(n_head):
            if d:
                send_back(d, k).wait_recv()
            put = jnp.where(slot_col == head_at(-d) * CAP + iota((local, CAP), 1), 1.0, 0.0)
            total += jnp.dot(put.astype(BF16), back_in[d, :, span(k)], preferred_element_type=F32)
        grad_ref[:, span(k)] = total.astype(BF16)
        return carry

    lax.fori_loop(0, chunks, finish, 0)

    def drain(k, carry):
        for d in range(1, n_head):
            send_row(d, k).wait_send()
            send_back(d, k).wait_send()
        for d in range(1, n_chip):
            spread(d, k, my_place).wait_send()
            send_sum(d, k).wait_send()
        for d in range(n_chip):
            share(d, k, core * n_chip + (chip - d + n_chip) % n_chip).wait_send()
        send_pair(k).wait_send()
        return carry

    lax.fori_loop(0, chunks, drain, 0)
    for d in range(1, n_head):
        send_meta(d).wait_send()
        send_loss(d).wait_send()
    for d in range(1, n_vocab):
        send_all(d, my_place).wait_send()
        send_stat(d, my_place).wait_send()


def per_device(n_head, n_vocab, hidden_states, head_weight, tags, targets, row_grad):
    local, depth = hidden_states.shape
    columns = head_weight.shape[2]
    own = n_head * CAP
    n_chip = n_vocab // 2
    group = n_vocab * own
    chunks = CHUNKS
    width = depth // chunks
    meta = jnp.stack([tags[:, 0].astype(F32), targets.astype(F32), row_grad.astype(F32)])
    vmem = pl.BlockSpec(memory_space=pltpu.VMEM)
    dma = pltpu.SemaphoreType.DMA
    loss, grad = pl.pallas_call(
        functools.partial(kernel, n_head, n_vocab, chunks),
        out_shape=(
            jax.ShapeDtypeStruct((1, local), F32),
            jax.ShapeDtypeStruct((local, depth), BF16),
        ),
        in_specs=[vmem, vmem, pl.BlockSpec(memory_space=pl.ANY)],
        out_specs=(vmem, vmem),
        scratch_shapes=[
            pltpu.VMEM((depth, columns), BF16),
            pltpu.VMEM((n_head, CAP, depth), BF16),
            pltpu.VMEM((n_head, CAP, depth), BF16),
            pltpu.VMEM((n_vocab, own, depth), BF16),
            pltpu.VMEM((n_head, own, 128), F32),
            pltpu.VMEM((n_head, own, 128), F32),
            pltpu.VMEM((n_vocab, own, 128), F32),
            pltpu.VMEM((group, columns), F32),
            pltpu.VMEM((group, columns), BF16),
            pltpu.VMEM((n_vocab, 8, group), F32),
            pltpu.VMEM((2, 2, n_chip, own, width), F32),
            pltpu.VMEM((n_chip, own, depth), BF16),
            pltpu.VMEM((n_chip, own, depth), BF16),
            pltpu.VMEM((n_chip, own, depth), BF16),
            pltpu.VMEM((n_chip, own, depth), BF16),
            pltpu.VMEM((n_head, CAP, depth), BF16),
            pltpu.VMEM((n_head, CAP, depth), BF16),
            pltpu.VMEM((own, 128), F32),
            pltpu.VMEM((n_head, own, 128), F32),
            dma((chunks,)),
            dma((n_head, chunks)), dma((n_head, chunks)),
            dma((n_head,)), dma((n_head,)),
            dma((n_chip, chunks)), dma((n_chip, chunks)),
            dma((n_chip, chunks)), dma((n_chip, chunks)),
            dma((n_vocab,)), dma((n_vocab,)),
            dma((n_vocab,)), dma((n_vocab,)),
            dma((chunks,)), dma((chunks,)),
            dma((n_chip, chunks)), dma((n_chip, chunks)),
            dma((n_head, chunks)), dma((n_head, chunks)),
            dma((n_head,)), dma((n_head,)),
        ],
        compiler_params=pltpu.CompilerParams(
            collective_id=0, has_side_effects=True, vmem_limit_bytes=56 * 1024 * 1024
        ),
    )(meta, hidden_states, head_weight)
    return loss[0].astype(BF16), grad


def solution(mesh):
    placed = (
        P(("head", "vocab"), None),
        P("head", None, "vocab"),
        P(("head", "vocab"), None),
        P(("head", "vocab")),
        P(("head", "vocab")),
    )
    return jax.shard_map(
        functools.partial(per_device, mesh.shape["head"], mesh.shape["vocab"]),
        mesh=mesh,
        in_specs=placed,
        out_specs=(P(("head", "vocab")), P(("head", "vocab"), None)),
        check_vma=False,
    )
```

```python
import functools

import jax
import jax.numpy as jnp
from jax import lax
from jax.experimental import pallas as pl
from jax.experimental.pallas import tpu as pltpu
from jax.sharding import PartitionSpec as P

CAP = 2
CHUNKS = 8
BATCHES = 4
MESH = pl.DeviceIdType.MESH
F32 = jnp.float32
BF16 = jnp.bfloat16


def iota(shape, dim):
    return lax.broadcasted_iota(jnp.int32, shape, dim).astype(F32)


def transposed(vector, axis):
    n = max(vector.shape)
    eye = iota((n, n), 0) == iota((n, n), 1)
    return jnp.sum(jnp.where(eye, vector, 0.0), axis=axis, keepdims=True)


def kernel(
    n_head, n_vocab, chunks, batches,
    tag_ref, target_ref, scale_ref, hidden_ref, w_hbm, loss_ref, grad_ref,
    w_ref, stage, row_out, row_in, rows, meta_out, meta_in, meta_all, logit_ref, dlog_ref,
    stat_all, part, pair_out, pair_in, sum_out, sum_in, back_out, back_in, loss_out, loss_in,
    w_sem, row_s, row_r, meta_s, meta_r, spread_s, spread_r, share_s, share_r,
    all_s, all_r, stat_s, stat_r, pair_s, pair_r, sum_s, sum_r, back_s, back_r, loss_s, loss_r,
):
    my_head, my_vocab = lax.axis_index("head"), lax.axis_index("vocab")
    n_chip = n_vocab // 2
    chip, core = my_vocab // 2, my_vocab % 2
    own = n_head * CAP
    local, depth = hidden_ref.shape
    width = depth // chunks
    wide = depth // batches
    group = n_vocab * own
    columns = w_ref.shape[1]

    def span(k):
        return pl.ds(pl.multiple_of(k * width, width), width)

    def wide_span(k):
        return pl.ds(pl.multiple_of(k * wide, wide), wide)

    def load_weight(k):
        return pltpu.make_async_copy(w_hbm.at[0, span(k)], w_ref.at[span(k)], w_sem.at[k])

    for k in range(chunks):
        load_weight(k).start()

    def head_peer(d):
        return ((my_head + d + n_head) % n_head, my_vocab)

    def vocab_peer(d):
        return (my_head, (my_vocab + d) % n_vocab)

    def chip_peer(d):
        return (my_head, ((chip + d) % n_chip) * 2 + core)

    partner = (my_head, chip * 2 + 1 - core)
    my_place = core * n_chip + chip

    def remote(src, dst, send, recv, device):
        return pltpu.make_async_remote_copy(
            src_ref=src, dst_ref=dst, send_sem=send, recv_sem=recv,
            device_id=device, device_id_type=MESH,
        )

    def whole(ref, count, send, recv, cut=None):
        view = ref.at[pl.ds(0, count)] if cut is None else ref.at[pl.ds(0, count), :, cut]
        return remote(view, view, send, recv, partner)

    barrier = pltpu.get_barrier_semaphore()
    for d in range(1, n_head):
        pl.semaphore_signal(barrier, inc=1, device_id=head_peer(d), device_id_type=MESH)
    for d in range(1, n_vocab):
        pl.semaphore_signal(barrier, inc=1, device_id=vocab_peer(d), device_id_type=MESH)

    tag_col = tag_ref[...].astype(F32)
    tag_row = transposed(tag_col, 0)
    target_row = target_ref[...].astype(F32)
    scale_row = scale_ref[...].astype(F32)
    earlier = (tag_col == tag_row) & (iota((local, local), 0) < iota((local, local), 1))
    rank_row = jnp.sum(jnp.where(earlier, 1.0, 0.0), axis=0, keepdims=True)
    slot_row = tag_row * CAP + rank_row
    slot_col = transposed(slot_row, 1)
    home = my_head.astype(F32)

    def wanted(seat):
        distance = jnp.floor(seat * (1.0 / CAP))
        head = home + distance
        head = jnp.where(head >= n_head, head - n_head, head)
        return head * CAP + seat - distance * CAP

    full = slot_row == wanted(iota((own, local), 0))
    picked = jnp.dot(
        jnp.where(full, 1.0, 0.0).astype(BF16), hidden_ref[...], preferred_element_type=F32
    )
    stage[...] = picked
    for d in range(n_head):
        piece = stage[d * CAP : (d + 1) * CAP, :].astype(BF16)
        (row_out if d else row_in)[d] = piece
    goal = jnp.sum(jnp.where(full, target_row, 0.0), axis=1, keepdims=True)
    scale = jnp.sum(jnp.where(full, scale_row, 0.0), axis=1, keepdims=True)
    lane, line = iota((own, 128), 1), iota((own, 128), 0)
    tile = jnp.where(lane == 0, goal, jnp.where(lane == 1, scale, 0.0))
    for d in range(n_head):
        kept = jnp.where((line >= d * CAP) & (line < (d + 1) * CAP), tile, 0.0)
        (meta_out if d else meta_in)[d] = kept

    pl.semaphore_wait(barrier, n_head + n_vocab - 2)

    for k in range(batches):
        for d in range(1, n_head):
            remote(row_out.at[d, :, wide_span(k)], row_in.at[d, :, wide_span(k)],
                   row_s, row_r.at[k], head_peer(d)).start()
        if k == 0:
            for d in range(1, n_head):
                remote(meta_out.at[d], meta_in.at[d], meta_s, meta_r, head_peer(d)).start()

    def gather_rows(k, carry):
        cut = wide_span(k)
        whole(row_in, n_head - 1, row_s, row_r.at[k], cut).wait_recv()
        for d in range(n_head):
            stage[d * CAP : (d + 1) * CAP, cut] = row_in[d, :, cut].astype(F32)
        rows[my_place, :, cut] = stage[:, cut].astype(BF16)
        block = rows.at[my_place, :, cut]
        for d in range(1, n_chip):
            remote(block, block, spread_s, spread_r.at[k], chip_peer(d)).start()
        return carry

    lax.fori_loop(0, batches, gather_rows, 0)

    whole(meta_in, n_head - 1, meta_s, meta_r).wait_recv()
    meta_all[my_place] = jnp.sum(meta_in[...], axis=0)
    for d in range(1, n_vocab):
        remote(meta_all.at[my_place], meta_all.at[my_place], all_s, all_r, vocab_peer(d)).start()

    logit_ref[...] = jnp.zeros_like(logit_ref)

    def forward_share(k):
        cut = wide_span(k)
        whole(rows, n_chip - 1, spread_s, spread_r.at[k], cut).wait_recv()
        half = rows.at[pl.ds(core * n_chip, n_chip), :, cut]
        remote(half, half, share_s, share_r.at[k], partner).start()

    forward_share(0)

    def multiply(k, carry):
        @pl.when(k + 1 < batches)
        def _():
            forward_share(k + 1)

        whole(rows, n_chip, share_s, share_r.at[k], wide_span(k)).wait_recv()
        for i in range(chunks // batches):
            j = k * (chunks // batches) + i
            load_weight(j).wait()
            x = rows[:, :, span(j)].reshape(group, width)
            logit_ref[...] += jnp.dot(x, w_ref[span(j), :], preferred_element_type=F32)
        return carry

    lax.fori_loop(0, batches, multiply, 0)

    whole(meta_all, n_vocab - 1, all_s, all_r).wait_recv()
    info = meta_all[...].reshape(group, 128)
    goal_col = info[:, 0:1] - (my_vocab * columns).astype(F32)
    scale_col = info[:, 1:2]
    logits = logit_ref[...]
    hit = iota((group, columns), 1) == goal_col
    top_col = jnp.max(logits, axis=1, keepdims=True)
    target_col = jnp.sum(jnp.where(hit, logits, 0.0), axis=1, keepdims=True)
    grown = jnp.exp(logits - top_col)
    logit_ref[...] = grown
    total_col = jnp.sum(grown, axis=1, keepdims=True)
    line = iota((8, group), 0)
    stat_all[my_place] = jnp.where(
        line == 0, transposed(top_col, 0),
        jnp.where(line == 1, transposed(total_col, 0), transposed(target_col, 0)),
    )
    for d in range(1, n_vocab):
        remote(stat_all.at[my_place], stat_all.at[my_place], stat_s, stat_r, vocab_peer(d)).start()
    whole(stat_all, n_vocab - 1, stat_s, stat_r).wait_recv()
    tops = stat_all[:, 0, :]
    row_top = jnp.max(tops, axis=0, keepdims=True)
    row_total = jnp.sum(stat_all[:, 1, :] * jnp.exp(tops - row_top), axis=0, keepdims=True)
    factor_col = scale_col * jnp.exp(top_col - transposed(row_top, 1)) / transposed(row_total, 1)
    hit = iota((group, columns), 1) == goal_col
    dlog_ref[...] = (logit_ref[...] * factor_col - jnp.where(hit, scale_col, 0.0)).astype(BF16)

    row_target = jnp.sum(stat_all[:, 2, :], axis=0, keepdims=True)
    loss_row = jnp.log(row_total) + row_top - row_target
    mine = iota((own, group), 1) == iota((own, group), 0) + (my_place * own).astype(F32)
    loss_col = jnp.sum(jnp.where(mine, loss_row, 0.0), axis=1, keepdims=True)
    loss_out[...] = jnp.broadcast_to(loss_col, (own, 128))
    for d in range(1, n_head):
        remote(loss_out, loss_in.at[d], loss_s, loss_r, head_peer(-d)).start()

    give_back = slot_col == wanted(iota((local, own), 1))
    give_back = jnp.where(give_back, 1.0, 0.0).astype(BF16)

    def back(k, carry):
        @pl.when(k < chunks)
        def _():
            value = lax.dot_general(
                dlog_ref[...], w_ref[span(k), :], (((1,), (1,)), ((), ())),
                preferred_element_type=F32,
            )
            part[k % 2] = value.reshape(2, n_chip, own, width)
            pair_out[:, :, span(k)] = part[k % 2, 1 - core].astype(BF16)
            remote(pair_out.at[:, :, span(k)], pair_in.at[:, :, span(k)],
                   pair_s, pair_r.at[k], partner).start()

        @pl.when((k >= 1) & (k < chunks + 1))
        def _():
            j = k - 1
            whole(pair_in, n_chip, pair_s, pair_r.at[j], span(j)).wait_recv()
            for d in range(1, n_chip):
                to = (chip + d) % n_chip
                both = part[j % 2, core, to] + pair_in[to, :, span(j)].astype(F32)
                sum_out[d, :, span(j)] = both.astype(BF16)
                remote(sum_out.at[d, :, span(j)], sum_in.at[d, :, span(j)],
                       sum_s, sum_r.at[j], chip_peer(d)).start()
            both = part[j % 2, core, chip] + pair_in[chip, :, span(j)].astype(F32)
            sum_in[0, :, span(j)] = both.astype(BF16)

        @pl.when((k >= 2) & (k < chunks + 2))
        def _():
            j = k - 2
            whole(sum_in, n_chip - 1, sum_s, sum_r.at[j], span(j)).wait_recv()
            stage[:, span(j)] = jnp.sum(sum_in[:, :, span(j)].astype(F32), axis=0)
            for d in range(n_head):
                piece = stage[d * CAP : (d + 1) * CAP, span(j)].astype(BF16)
                (back_out if d else back_in)[d, :, span(j)] = piece
                if d:
                    remote(back_out.at[d, :, span(j)], back_in.at[d, :, span(j)],
                           back_s, back_r.at[j], head_peer(-d)).start()

        @pl.when(k >= 4)
        def _():
            j = k - 4
            whole(back_in, n_head - 1, back_s, back_r.at[j], span(j)).wait_recv()
            for d in range(n_head):
                stage[d * CAP : (d + 1) * CAP, span(j)] = back_in[d, :, span(j)].astype(F32)
            grad_ref[:, span(j)] = jnp.dot(
                give_back, stage[:, span(j)].astype(BF16), preferred_element_type=F32
            ).astype(BF16)

        return carry

    lax.fori_loop(0, chunks + 4, back, 0)

    whole(loss_in, n_head - 1, loss_s, loss_r).wait_recv()
    loss = jnp.zeros((1, local), F32)
    for d in range(n_head):
        tile = loss_in[d] if d else loss_out[...]
        there = home + d
        there = jnp.where(there >= n_head, there - n_head, there)
        mask = (tag_row == there) & (iota((own, local), 0) == d * CAP + rank_row)
        loss += jnp.sum(jnp.where(mask, tile[:, :local], 0.0), axis=0, keepdims=True)
    loss_ref[...] = loss.astype(BF16)

    whole(row_out, n_head - 1, row_s, row_r.at[0]).wait_send()
    whole(back_out, n_head - 1, back_s, back_r.at[0]).wait_send()
    whole(meta_out, n_head - 1, meta_s, meta_r).wait_send()
    whole(loss_in, n_head - 1, loss_s, loss_r).wait_send()
    whole(rows, n_chip - 1, spread_s, spread_r.at[0]).wait_send()
    whole(rows, n_chip, share_s, share_r.at[0]).wait_send()
    whole(pair_out, n_chip, pair_s, pair_r.at[0]).wait_send()
    whole(sum_out, n_chip - 1, sum_s, sum_r.at[0]).wait_send()
    whole(meta_all, n_vocab - 1, all_s, all_r).wait_send()
    whole(stat_all, n_vocab - 1, stat_s, stat_r).wait_send()


def per_device(n_head, n_vocab, hidden_states, head_weight, tags, targets, row_grad):
    local, depth = hidden_states.shape
    columns = head_weight.shape[2]
    own = n_head * CAP
    n_chip = n_vocab // 2
    group = n_vocab * own
    chunks = CHUNKS
    width = depth // chunks
    vmem = pl.BlockSpec(memory_space=pltpu.VMEM)
    dma = pltpu.SemaphoreType.DMA
    loss, grad = pl.pallas_call(
        functools.partial(kernel, n_head, n_vocab, chunks, BATCHES),
        out_shape=(
            jax.ShapeDtypeStruct((1, local), BF16),
            jax.ShapeDtypeStruct((local, depth), BF16),
        ),
        in_specs=[vmem, vmem, vmem, vmem, pl.BlockSpec(memory_space=pl.ANY)],
        out_specs=(vmem, vmem),
        scratch_shapes=[
            pltpu.VMEM((depth, columns), BF16),
            pltpu.VMEM((own, depth), F32),
            pltpu.VMEM((n_head, CAP, depth), BF16),
            pltpu.VMEM((n_head, CAP, depth), BF16),
            pltpu.VMEM((n_vocab, own, depth), BF16),
            pltpu.VMEM((n_head, own, 128), F32),
            pltpu.VMEM((n_head, own, 128), F32),
            pltpu.VMEM((n_vocab, own, 128), F32),
            pltpu.VMEM((group, columns), F32),
            pltpu.VMEM((group, columns), BF16),
            pltpu.VMEM((n_vocab, 8, group), F32),
            pltpu.VMEM((2, 2, n_chip, own, width), F32),
            pltpu.VMEM((n_chip, own, depth), BF16),
            pltpu.VMEM((n_chip, own, depth), BF16),
            pltpu.VMEM((n_chip, own, depth), BF16),
            pltpu.VMEM((n_chip, own, depth), BF16),
            pltpu.VMEM((n_head, CAP, depth), BF16),
            pltpu.VMEM((n_head, CAP, depth), BF16),
            pltpu.VMEM((own, 128), F32),
            pltpu.VMEM((n_head, own, 128), F32),
            dma((chunks,)),
            dma, dma((BATCHES,)),
            dma, dma,
            dma, dma((BATCHES,)),
            dma, dma((BATCHES,)),
            dma, dma,
            dma, dma,
            dma, dma((chunks,)),
            dma, dma((chunks,)),
            dma, dma((chunks,)),
            dma, dma,
        ],
        compiler_params=pltpu.CompilerParams(
            collective_id=0, has_side_effects=True, vmem_limit_bytes=56 * 1024 * 1024
        ),
    )(tags, targets.reshape(1, local), row_grad.reshape(1, local), hidden_states, head_weight)
    return loss.reshape(local), grad


def solution(mesh):
    placed = (
        P(("head", "vocab"), None),
        P("head", None, "vocab"),
        P(("head", "vocab"), None),
        P(("head", "vocab")),
        P(("head", "vocab")),
    )
    return jax.shard_map(
        functools.partial(per_device, mesh.shape["head"], mesh.shape["vocab"]),
        mesh=mesh,
        in_specs=placed,
        out_specs=(P(("head", "vocab")), P(("head", "vocab"), None)),
        check_vma=False,
    )
```

```python
import functools

import jax
import jax.numpy as jnp
from jax import lax
from jax.experimental import pallas as pl
from jax.experimental.pallas import tpu as pltpu
from jax.sharding import PartitionSpec as P

CAP = 2
CHUNKS = 8
BATCHES = 4
MESH = pl.DeviceIdType.MESH
F32 = jnp.float32
BF16 = jnp.bfloat16


def iota(shape, dim):
    return lax.broadcasted_iota(jnp.int32, shape, dim).astype(F32)


def transposed(vector, axis):
    n = max(vector.shape)
    eye = iota((n, n), 0) == iota((n, n), 1)
    return jnp.sum(jnp.where(eye, vector, 0.0), axis=axis, keepdims=True)


def kernel(
    n_head, n_vocab, chunks, batches,
    tag_ref, target_ref, scale_ref, hidden_ref, w_hbm, loss_ref, grad_ref,
    w_ref, stage, row_out, row_in, rows, meta_out, meta_in, meta_all, logit_ref, dlog_ref,
    stat_all, part, pair_out, pair_in, sum_out, sum_in, back_out, back_in, loss_out, loss_in,
    w_sem, row_s, row_r, meta_s, meta_r, spread_s, spread_r, share_s, share_r,
    all_s, all_r, stat_s, stat_r, pair_s, pair_r, sum_s, sum_r, back_s, back_r, loss_s, loss_r,
):
    my_head, my_vocab = lax.axis_index("head"), lax.axis_index("vocab")
    n_chip = n_vocab // 2
    chip, core = my_vocab // 2, my_vocab % 2
    own = n_head * CAP
    local, depth = hidden_ref.shape
    width = depth // chunks
    wide = depth // batches
    group = n_vocab * own
    columns = w_ref.shape[1]

    def span(k):
        return pl.ds(pl.multiple_of(k * width, width), width)

    def wide_span(k):
        return pl.ds(pl.multiple_of(k * wide, wide), wide)

    def load_weight(k):
        return pltpu.make_async_copy(w_hbm.at[0, span(k)], w_ref.at[span(k)], w_sem.at[k])

    for k in range(chunks):
        load_weight(k).start()

    def head_peer(d):
        return ((my_head + d + n_head) % n_head, my_vocab)

    def vocab_peer(d):
        return (my_head, (my_vocab + d) % n_vocab)

    def chip_peer(d):
        return (my_head, ((chip + d) % n_chip) * 2 + core)

    partner = (my_head, chip * 2 + 1 - core)
    my_place = core * n_chip + chip

    def remote(src, dst, send, recv, device):
        return pltpu.make_async_remote_copy(
            src_ref=src, dst_ref=dst, send_sem=send, recv_sem=recv,
            device_id=device, device_id_type=MESH,
        )

    def whole(ref, count, send, recv, cut=None):
        view = ref.at[pl.ds(0, count)] if cut is None else ref.at[pl.ds(0, count), :, cut]
        return remote(view, view, send, recv, partner)

    barrier = pltpu.get_barrier_semaphore()
    for d in range(1, n_head):
        pl.semaphore_signal(barrier, inc=1, device_id=head_peer(d), device_id_type=MESH)
    for d in range(1, n_vocab):
        pl.semaphore_signal(barrier, inc=1, device_id=vocab_peer(d), device_id_type=MESH)

    tag_row = tag_ref[...].astype(F32)
    tag_col = transposed(tag_row, 1)
    target_row = target_ref[...].astype(F32)
    scale_row = scale_ref[...].astype(F32)
    earlier = (tag_col == tag_row) & (iota((local, local), 0) < iota((local, local), 1))
    rank_row = jnp.sum(jnp.where(earlier, 1.0, 0.0), axis=0, keepdims=True)
    slot_row = tag_row * CAP + rank_row
    slot_col = transposed(slot_row, 1)
    home = my_head.astype(F32)

    def wanted(seat):
        distance = jnp.floor(seat * (1.0 / CAP))
        head = home + distance
        head = jnp.where(head >= n_head, head - n_head, head)
        return head * CAP + seat - distance * CAP

    full = slot_row == wanted(iota((own, local), 0))
    picked = jnp.dot(
        jnp.where(full, 1.0, 0.0).astype(BF16), hidden_ref[...], preferred_element_type=F32
    )
    stage[...] = picked
    for d in range(n_head):
        piece = stage[d * CAP : (d + 1) * CAP, :].astype(BF16)
        (row_out if d else row_in)[d] = piece
    goal = jnp.sum(jnp.where(full, target_row, 0.0), axis=1, keepdims=True)
    scale = jnp.sum(jnp.where(full, scale_row, 0.0), axis=1, keepdims=True)
    lane, line = iota((own, 128), 1), iota((own, 128), 0)
    tile = jnp.where(lane == 0, goal, jnp.where(lane == 1, scale, 0.0))
    for d in range(n_head):
        kept = jnp.where((line >= d * CAP) & (line < (d + 1) * CAP), tile, 0.0)
        (meta_out if d else meta_in)[d] = kept

    pl.semaphore_wait(barrier, n_head + n_vocab - 2)

    for k in range(batches):
        for d in range(1, n_head):
            remote(row_out.at[d, :, wide_span(k)], row_in.at[d, :, wide_span(k)],
                   row_s, row_r.at[k], head_peer(d)).start()
        if k == 0:
            for d in range(1, n_head):
                remote(meta_out.at[d], meta_in.at[d], meta_s, meta_r, head_peer(d)).start()

    def gather_rows(k, carry):
        cut = wide_span(k)
        whole(row_in, n_head - 1, row_s, row_r.at[k], cut).wait_recv()
        for d in range(n_head):
            stage[d * CAP : (d + 1) * CAP, cut] = row_in[d, :, cut].astype(F32)
        rows[my_place, :, cut] = stage[:, cut].astype(BF16)
        block = rows.at[my_place, :, cut]
        for d in range(1, n_chip):
            remote(block, block, spread_s, spread_r.at[k], chip_peer(d)).start()
        return carry

    lax.fori_loop(0, batches, gather_rows, 0)

    whole(meta_in, n_head - 1, meta_s, meta_r).wait_recv()
    meta_all[my_place] = jnp.sum(meta_in[...], axis=0)
    for d in range(1, n_vocab):
        remote(meta_all.at[my_place], meta_all.at[my_place], all_s, all_r, vocab_peer(d)).start()

    logit_ref[...] = jnp.zeros_like(logit_ref)

    def forward_share(k):
        cut = wide_span(k)
        whole(rows, n_chip - 1, spread_s, spread_r.at[k], cut).wait_recv()
        half = rows.at[pl.ds(core * n_chip, n_chip), :, cut]
        remote(half, half, share_s, share_r.at[k], partner).start()

    forward_share(0)

    def multiply(k, carry):
        @pl.when(k + 1 < batches)
        def _():
            forward_share(k + 1)

        whole(rows, n_chip, share_s, share_r.at[k], wide_span(k)).wait_recv()
        for i in range(chunks // batches):
            j = k * (chunks // batches) + i
            load_weight(j).wait()
            x = rows[:, :, span(j)].reshape(group, width)
            logit_ref[...] += jnp.dot(x, w_ref[span(j), :], preferred_element_type=F32)
        return carry

    lax.fori_loop(0, batches, multiply, 0)

    whole(meta_all, n_vocab - 1, all_s, all_r).wait_recv()
    info = meta_all[...].reshape(group, 128)
    goal_col = info[:, 0:1] - (my_vocab * columns).astype(F32)
    scale_col = info[:, 1:2]
    logits = logit_ref[...]
    hit = iota((group, columns), 1) == goal_col
    top_col = jnp.max(logits, axis=1, keepdims=True)
    target_col = jnp.sum(jnp.where(hit, logits, 0.0), axis=1, keepdims=True)
    grown = jnp.exp(logits - top_col)
    logit_ref[...] = grown
    total_col = jnp.sum(grown, axis=1, keepdims=True)
    line = iota((8, group), 0)
    stat_all[my_place] = jnp.where(
        line == 0, transposed(top_col, 0),
        jnp.where(line == 1, transposed(total_col, 0), transposed(target_col, 0)),
    )
    for d in range(1, n_vocab):
        remote(stat_all.at[my_place], stat_all.at[my_place], stat_s, stat_r, vocab_peer(d)).start()
    whole(stat_all, n_vocab - 1, stat_s, stat_r).wait_recv()
    tops = stat_all[:, 0, :]
    row_top = jnp.max(tops, axis=0, keepdims=True)
    row_total = jnp.sum(stat_all[:, 1, :] * jnp.exp(tops - row_top), axis=0, keepdims=True)
    factor_col = scale_col * jnp.exp(top_col - transposed(row_top, 1)) / transposed(row_total, 1)
    hit = iota((group, columns), 1) == goal_col
    dlog_ref[...] = (logit_ref[...] * factor_col - jnp.where(hit, scale_col, 0.0)).astype(BF16)

    row_target = jnp.sum(stat_all[:, 2, :], axis=0, keepdims=True)
    loss_row = jnp.log(row_total) + row_top - row_target
    mine = iota((own, group), 1) == iota((own, group), 0) + (my_place * own).astype(F32)
    loss_col = jnp.sum(jnp.where(mine, loss_row, 0.0), axis=1, keepdims=True)
    loss_out[...] = jnp.broadcast_to(loss_col, (own, 128))
    for d in range(1, n_head):
        remote(loss_out, loss_in.at[d], loss_s, loss_r, head_peer(-d)).start()

    give_back = slot_col == wanted(iota((local, own), 1))
    give_back = jnp.where(give_back, 1.0, 0.0).astype(BF16)

    def back(k, carry):
        @pl.when(k < chunks)
        def _():
            value = lax.dot_general(
                w_ref[span(k), :], dlog_ref[...], (((1,), (1,)), ((), ())),
                preferred_element_type=F32,
            )
            part[k % 2] = value.T.reshape(2, n_chip, own, width)
            pair_out[:, :, span(k)] = part[k % 2, 1 - core].astype(BF16)
            remote(pair_out.at[:, :, span(k)], pair_in.at[:, :, span(k)],
                   pair_s, pair_r.at[k], partner).start()

        @pl.when((k >= 1) & (k < chunks + 1))
        def _():
            j = k - 1
            whole(pair_in, n_chip, pair_s, pair_r.at[j], span(j)).wait_recv()
            for d in range(1, n_chip):
                to = (chip + d) % n_chip
                both = part[j % 2, core, to] + pair_in[to, :, span(j)].astype(F32)
                sum_out[d, :, span(j)] = both.astype(BF16)
                remote(sum_out.at[d, :, span(j)], sum_in.at[d, :, span(j)],
                       sum_s, sum_r.at[j], chip_peer(d)).start()
            both = part[j % 2, core, chip] + pair_in[chip, :, span(j)].astype(F32)
            sum_in[0, :, span(j)] = both.astype(BF16)

        @pl.when((k >= 2) & (k < chunks + 2))
        def _():
            j = k - 2
            whole(sum_in, n_chip - 1, sum_s, sum_r.at[j], span(j)).wait_recv()
            stage[:, span(j)] = jnp.sum(sum_in[:, :, span(j)].astype(F32), axis=0)
            for d in range(n_head):
                piece = stage[d * CAP : (d + 1) * CAP, span(j)].astype(BF16)
                (back_out if d else back_in)[d, :, span(j)] = piece
                if d:
                    remote(back_out.at[d, :, span(j)], back_in.at[d, :, span(j)],
                           back_s, back_r.at[j], head_peer(-d)).start()

        @pl.when(k >= 4)
        def _():
            j = k - 4
            whole(back_in, n_head - 1, back_s, back_r.at[j], span(j)).wait_recv()
            for d in range(n_head):
                stage[d * CAP : (d + 1) * CAP, span(j)] = back_in[d, :, span(j)].astype(F32)
            grad_ref[:, span(j)] = jnp.dot(
                give_back, stage[:, span(j)].astype(BF16), preferred_element_type=F32
            ).astype(BF16)

        return carry

    lax.fori_loop(0, chunks + 4, back, 0)

    whole(loss_in, n_head - 1, loss_s, loss_r).wait_recv()
    loss = jnp.zeros((1, local), F32)
    for d in range(n_head):
        tile = loss_in[d] if d else loss_out[...]
        there = home + d
        there = jnp.where(there >= n_head, there - n_head, there)
        mask = (tag_row == there) & (iota((own, local), 0) == d * CAP + rank_row)
        loss += jnp.sum(jnp.where(mask, tile[:, :local], 0.0), axis=0, keepdims=True)
    loss_ref[...] = loss.astype(BF16)

    whole(row_out, n_head - 1, row_s, row_r.at[0]).wait_send()
    whole(back_out, n_head - 1, back_s, back_r.at[0]).wait_send()
    whole(meta_out, n_head - 1, meta_s, meta_r).wait_send()
    whole(loss_in, n_head - 1, loss_s, loss_r).wait_send()
    whole(rows, n_chip - 1, spread_s, spread_r.at[0]).wait_send()
    whole(rows, n_chip, share_s, share_r.at[0]).wait_send()
    whole(pair_out, n_chip, pair_s, pair_r.at[0]).wait_send()
    whole(sum_out, n_chip - 1, sum_s, sum_r.at[0]).wait_send()
    whole(meta_all, n_vocab - 1, all_s, all_r).wait_send()
    whole(stat_all, n_vocab - 1, stat_s, stat_r).wait_send()


def hand_over(loss_in, grad_in, loss_ref, grad_ref):
    loss_ref[...] = loss_in[...]
    grad_ref[...] = grad_in[...]


def per_device(n_head, n_vocab, hidden_states, head_weight, tags, targets, row_grad):
    local, depth = hidden_states.shape
    columns = head_weight.shape[2]
    own = n_head * CAP
    n_chip = n_vocab // 2
    group = n_vocab * own
    chunks = CHUNKS
    width = depth // chunks
    vmem = pl.BlockSpec(memory_space=pltpu.VMEM)
    dma = pltpu.SemaphoreType.DMA
    loss, grad = pl.pallas_call(
        functools.partial(kernel, n_head, n_vocab, chunks, BATCHES),
        out_shape=(
            jax.ShapeDtypeStruct((1, local), BF16),
            jax.ShapeDtypeStruct((local, depth), BF16),
        ),
        in_specs=[vmem, vmem, vmem, vmem, pl.BlockSpec(memory_space=pl.ANY)],
        out_specs=(vmem, vmem),
        scratch_shapes=[
            pltpu.VMEM((depth, columns), BF16),
            pltpu.VMEM((own, depth), F32),
            pltpu.VMEM((n_head, CAP, depth), BF16),
            pltpu.VMEM((n_head, CAP, depth), BF16),
            pltpu.VMEM((n_vocab, own, depth), BF16),
            pltpu.VMEM((n_head, own, 128), F32),
            pltpu.VMEM((n_head, own, 128), F32),
            pltpu.VMEM((n_vocab, own, 128), F32),
            pltpu.VMEM((group, columns), F32),
            pltpu.VMEM((group, columns), BF16),
            pltpu.VMEM((n_vocab, 8, group), F32),
            pltpu.VMEM((2, 2, n_chip, own, width), F32),
            pltpu.VMEM((n_chip, own, depth), BF16),
            pltpu.VMEM((n_chip, own, depth), BF16),
            pltpu.VMEM((n_chip, own, depth), BF16),
            pltpu.VMEM((n_chip, own, depth), BF16),
            pltpu.VMEM((n_head, CAP, depth), BF16),
            pltpu.VMEM((n_head, CAP, depth), BF16),
            pltpu.VMEM((own, 128), F32),
            pltpu.VMEM((n_head, own, 128), F32),
            dma((chunks,)),
            dma, dma((BATCHES,)),
            dma, dma,
            dma, dma((BATCHES,)),
            dma, dma((BATCHES,)),
            dma, dma,
            dma, dma,
            dma, dma((chunks,)),
            dma, dma((chunks,)),
            dma, dma((chunks,)),
            dma, dma,
        ],
        compiler_params=pltpu.CompilerParams(
            collective_id=0, has_side_effects=True, vmem_limit_bytes=56 * 1024 * 1024
        ),
    )(tags.reshape(1, local), targets.reshape(1, local), row_grad.reshape(1, local), hidden_states, head_weight)
    loss, grad = pl.pallas_call(
        hand_over,
        out_shape=(
            jax.ShapeDtypeStruct((1, local), BF16),
            jax.ShapeDtypeStruct((local, depth), BF16),
        ),
        in_specs=[vmem, vmem],
        out_specs=(vmem, vmem),
    )(loss, grad)
    return loss.reshape(local), grad


def solution(mesh):
    placed = (
        P(("head", "vocab"), None),
        P("head", None, "vocab"),
        P(("head", "vocab"), None),
        P(("head", "vocab")),
        P(("head", "vocab")),
    )
    return jax.shard_map(
        functools.partial(per_device, mesh.shape["head"], mesh.shape["vocab"]),
        mesh=mesh,
        in_specs=placed,
        out_specs=(P(("head", "vocab")), P(("head", "vocab"), None)),
        check_vma=False,
    )
```

```python
import functools

import jax
import jax.numpy as jnp
from jax import lax
from jax.experimental import pallas as pl
from jax.experimental.pallas import tpu as pltpu
from jax.sharding import PartitionSpec as P

CAP = 2
CHUNKS = 8
BATCHES = 4
MESH = pl.DeviceIdType.MESH
F32 = jnp.float32
BF16 = jnp.bfloat16


def iota(shape, dim):
    return lax.broadcasted_iota(jnp.int32, shape, dim).astype(F32)


def transposed(vector, axis):
    n = max(vector.shape)
    eye = iota((n, n), 0) == iota((n, n), 1)
    return jnp.sum(jnp.where(eye, vector, 0.0), axis=axis, keepdims=True)


def kernel(
    n_head, n_vocab, chunks, batches,
    tag_ref, target_ref, scale_ref, hidden_ref, w_hbm, loss_ref, grad_ref,
    w_ref, stage, row_out, row_in, rows, meta_out, meta_in, meta_all, logit_ref, dlog_ref,
    stat_all, part, pair_out, pair_in, sum_out, sum_in, back_out, back_in, loss_out, loss_in,
    w_sem, row_s, row_r, meta_s, meta_r, spread_s, spread_r, share_s, share_r,
    all_s, all_r, stat_s, stat_r, pair_s, pair_r, sum_s, sum_r, back_s, back_r, loss_s, loss_r,
):
    my_head, my_vocab = lax.axis_index("head"), lax.axis_index("vocab")
    n_chip = n_vocab // 2
    chip, core = my_vocab // 2, my_vocab % 2
    own = n_head * CAP
    local, depth = hidden_ref.shape
    width = depth // chunks
    wide = depth // batches
    group = n_vocab * own
    columns = w_ref.shape[1]

    def narrow_span(k):
        return pl.ds(pl.multiple_of(k * width, width), width)

    def wide_span(k):
        return pl.ds(pl.multiple_of(k * wide, wide), wide)

    def load_weight(k):
        return pltpu.make_async_copy(w_hbm.at[0, narrow_span(k)], w_ref.at[narrow_span(k)], w_sem.at[k])

    for k in range(chunks):
        load_weight(k).start()

    def head_peer(d):
        return ((my_head + d + n_head) % n_head, my_vocab)

    def vocab_peer(d):
        return (my_head, (my_vocab + d) % n_vocab)

    def chip_peer(d):
        return (my_head, ((chip + d) % n_chip) * 2 + core)

    partner = (my_head, chip * 2 + 1 - core)
    my_place = core * n_chip + chip

    def remote(src, dst, send, recv, device):
        return pltpu.make_async_remote_copy(
            src_ref=src, dst_ref=dst, send_sem=send, recv_sem=recv,
            device_id=device, device_id_type=MESH,
        )

    def whole(ref, count, send, recv, cut=None):
        view = ref.at[pl.ds(0, count)] if cut is None else ref.at[pl.ds(0, count), :, cut]
        return remote(view, view, send, recv, partner)

    barrier = pltpu.get_barrier_semaphore()
    for d in range(1, n_head):
        pl.semaphore_signal(barrier, inc=1, device_id=head_peer(d), device_id_type=MESH)
    for d in range(1, n_vocab):
        pl.semaphore_signal(barrier, inc=1, device_id=vocab_peer(d), device_id_type=MESH)

    tag_row = tag_ref[...].astype(F32)
    tag_col = transposed(tag_row, 1)
    target_row = target_ref[...].astype(F32)
    scale_row = scale_ref[...].astype(F32)
    earlier = (tag_col == tag_row) & (iota((local, local), 0) < iota((local, local), 1))
    rank_row = jnp.sum(jnp.where(earlier, 1.0, 0.0), axis=0, keepdims=True)
    slot_row = tag_row * CAP + rank_row
    slot_col = transposed(slot_row, 1)
    home = my_head.astype(F32)

    def wanted(seat):
        distance = jnp.floor(seat * (1.0 / CAP))
        head = home + distance
        head = jnp.where(head >= n_head, head - n_head, head)
        return head * CAP + seat - distance * CAP

    full = slot_row == wanted(iota((own, local), 0))
    picked = jnp.dot(
        jnp.where(full, 1.0, 0.0).astype(BF16), hidden_ref[...], preferred_element_type=F32
    )
    stage[...] = picked
    for d in range(n_head):
        piece = stage[d * CAP : (d + 1) * CAP, :].astype(BF16)
        (row_out if d else row_in)[d] = piece
    goal = jnp.sum(jnp.where(full, target_row, 0.0), axis=1, keepdims=True)
    scale = jnp.sum(jnp.where(full, scale_row, 0.0), axis=1, keepdims=True)
    lane, line = iota((own, 128), 1), iota((own, 128), 0)
    tile = jnp.where(lane == 0, goal, jnp.where(lane == 1, scale, 0.0))
    for d in range(n_head):
        kept = jnp.where((line >= d * CAP) & (line < (d + 1) * CAP), tile, 0.0)
        (meta_out if d else meta_in)[d] = kept

    pl.semaphore_wait(barrier, n_head + n_vocab - 2)

    for k in range(batches):
        for d in range(1, n_head):
            remote(row_out.at[d, :, wide_span(k)], row_in.at[d, :, wide_span(k)],
                   row_s, row_r.at[k], head_peer(d)).start()
        if k == 0:
            for d in range(1, n_head):
                remote(meta_out.at[d], meta_in.at[d], meta_s, meta_r, head_peer(d)).start()

    def gather_rows(k, carry):
        cut = wide_span(k)
        whole(row_in, n_head - 1, row_s, row_r.at[k], cut).wait_recv()
        for d in range(n_head):
            stage[d * CAP : (d + 1) * CAP, cut] = row_in[d, :, cut].astype(F32)
        rows[my_place, :, cut] = stage[:, cut].astype(BF16)
        block = rows.at[my_place, :, cut]
        for d in range(1, n_chip):
            remote(block, block, spread_s, spread_r.at[k], chip_peer(d)).start()
        return carry

    lax.fori_loop(0, batches, gather_rows, 0)

    whole(meta_in, n_head - 1, meta_s, meta_r).wait_recv()
    meta_all[my_place] = jnp.sum(meta_in[...], axis=0)
    for d in range(1, n_vocab):
        remote(meta_all.at[my_place], meta_all.at[my_place], all_s, all_r, vocab_peer(d)).start()

    logit_ref[...] = jnp.zeros_like(logit_ref)

    def forward_share(k):
        cut = wide_span(k)
        whole(rows, n_chip - 1, spread_s, spread_r.at[k], cut).wait_recv()
        half = rows.at[pl.ds(core * n_chip, n_chip), :, cut]
        remote(half, half, share_s, share_r.at[k], partner).start()

    forward_share(0)

    def multiply(k, carry):
        @pl.when(k + 1 < batches)
        def _():
            forward_share(k + 1)

        whole(rows, n_chip, share_s, share_r.at[k], wide_span(k)).wait_recv()
        for i in range(chunks // batches):
            j = k * (chunks // batches) + i
            load_weight(j).wait()
            x = rows[:, :, narrow_span(j)].reshape(group, width)
            logit_ref[...] += jnp.dot(x, w_ref[narrow_span(j), :], preferred_element_type=F32)
        return carry

    lax.fori_loop(0, batches, multiply, 0)

    whole(meta_all, n_vocab - 1, all_s, all_r).wait_recv()
    info = meta_all[...].reshape(group, 128)
    goal_col = info[:, 0:1] - (my_vocab * columns).astype(F32)
    scale_col = info[:, 1:2]
    logits = logit_ref[...]
    hit = iota((group, columns), 1) == goal_col
    top_col = jnp.max(logits, axis=1, keepdims=True)
    target_col = jnp.sum(jnp.where(hit, logits, 0.0), axis=1, keepdims=True)
    grown = jnp.exp(logits - top_col)
    logit_ref[...] = grown
    total_col = jnp.sum(grown, axis=1, keepdims=True)
    line = iota((8, group), 0)
    stat_all[my_place] = jnp.where(
        line == 0, transposed(top_col, 0),
        jnp.where(line == 1, transposed(total_col, 0), transposed(target_col, 0)),
    )
    for d in range(1, n_vocab):
        remote(stat_all.at[my_place], stat_all.at[my_place], stat_s, stat_r, vocab_peer(d)).start()
    whole(stat_all, n_vocab - 1, stat_s, stat_r).wait_recv()
    tops = stat_all[:, 0, :]
    row_top = jnp.max(tops, axis=0, keepdims=True)
    row_total = jnp.sum(stat_all[:, 1, :] * jnp.exp(tops - row_top), axis=0, keepdims=True)
    factor_col = scale_col * jnp.exp(top_col - transposed(row_top, 1)) / transposed(row_total, 1)
    hit = iota((group, columns), 1) == goal_col
    dlog_ref[...] = (logit_ref[...] * factor_col - jnp.where(hit, scale_col, 0.0)).astype(BF16)

    row_target = jnp.sum(stat_all[:, 2, :], axis=0, keepdims=True)
    loss_row = jnp.log(row_total) + row_top - row_target
    mine = iota((own, group), 1) == iota((own, group), 0) + (my_place * own).astype(F32)
    loss_col = jnp.sum(jnp.where(mine, loss_row, 0.0), axis=1, keepdims=True)
    loss_out[...] = jnp.broadcast_to(loss_col, (own, 128))
    for d in range(1, n_head):
        remote(loss_out, loss_in.at[d], loss_s, loss_r, head_peer(-d)).start()

    give_back = slot_col == wanted(iota((local, own), 1))
    give_back = jnp.where(give_back, 1.0, 0.0).astype(BF16)

    def back(k, carry):
        @pl.when(k < batches)
        def _():
            value = lax.dot_general(
                w_ref[wide_span(k), :], dlog_ref[...], (((1,), (1,)), ((), ())),
                preferred_element_type=F32,
            )
            part[k % 2] = value.T.reshape(2, n_chip, own, wide)
            pair_out[:, :, wide_span(k)] = part[k % 2, 1 - core].astype(BF16)
            remote(pair_out.at[:, :, wide_span(k)], pair_in.at[:, :, wide_span(k)],
                   pair_s, pair_r.at[k], partner).start()

        @pl.when((k >= 1) & (k < batches + 1))
        def _():
            j = k - 1
            whole(pair_in, n_chip, pair_s, pair_r.at[j], wide_span(j)).wait_recv()
            for d in range(1, n_chip):
                to = (chip + d) % n_chip
                both = part[j % 2, core, to] + pair_in[to, :, wide_span(j)].astype(F32)
                sum_out[d, :, wide_span(j)] = both.astype(BF16)
                remote(sum_out.at[d, :, wide_span(j)], sum_in.at[d, :, wide_span(j)],
                       sum_s, sum_r.at[j], chip_peer(d)).start()
            both = part[j % 2, core, chip] + pair_in[chip, :, wide_span(j)].astype(F32)
            sum_in[0, :, wide_span(j)] = both.astype(BF16)

        @pl.when((k >= 2) & (k < batches + 2))
        def _():
            j = k - 2
            whole(sum_in, n_chip - 1, sum_s, sum_r.at[j], wide_span(j)).wait_recv()
            stage[:, wide_span(j)] = jnp.sum(sum_in[:, :, wide_span(j)].astype(F32), axis=0)
            for d in range(n_head):
                piece = stage[d * CAP : (d + 1) * CAP, wide_span(j)].astype(BF16)
                (back_out if d else back_in)[d, :, wide_span(j)] = piece
                if d:
                    remote(back_out.at[d, :, wide_span(j)], back_in.at[d, :, wide_span(j)],
                           back_s, back_r.at[j], head_peer(-d)).start()

        @pl.when(k >= 3)
        def _():
            j = k - 3
            whole(back_in, n_head - 1, back_s, back_r.at[j], wide_span(j)).wait_recv()
            for d in range(n_head):
                stage[d * CAP : (d + 1) * CAP, wide_span(j)] = back_in[d, :, wide_span(j)].astype(F32)
            grad_ref[:, wide_span(j)] = jnp.dot(
                give_back, stage[:, wide_span(j)].astype(BF16), preferred_element_type=F32
            ).astype(BF16)

        return carry

    lax.fori_loop(0, batches + 3, back, 0)

    whole(loss_in, n_head - 1, loss_s, loss_r).wait_recv()
    loss = jnp.zeros((1, local), F32)
    for d in range(n_head):
        tile = loss_in[d] if d else loss_out[...]
        there = home + d
        there = jnp.where(there >= n_head, there - n_head, there)
        mask = (tag_row == there) & (iota((own, local), 0) == d * CAP + rank_row)
        loss += jnp.sum(jnp.where(mask, tile[:, :local], 0.0), axis=0, keepdims=True)
    loss_ref[...] = loss.astype(BF16)

    whole(row_out, n_head - 1, row_s, row_r.at[0]).wait_send()
    whole(back_out, n_head - 1, back_s, back_r.at[0]).wait_send()
    whole(meta_out, n_head - 1, meta_s, meta_r).wait_send()
    whole(loss_in, n_head - 1, loss_s, loss_r).wait_send()
    whole(rows, n_chip - 1, spread_s, spread_r.at[0]).wait_send()
    whole(rows, n_chip, share_s, share_r.at[0]).wait_send()
    whole(pair_out, n_chip, pair_s, pair_r.at[0]).wait_send()
    whole(sum_out, n_chip - 1, sum_s, sum_r.at[0]).wait_send()
    whole(meta_all, n_vocab - 1, all_s, all_r).wait_send()
    whole(stat_all, n_vocab - 1, stat_s, stat_r).wait_send()


def hand_over(loss_in, grad_in, loss_ref, grad_ref):
    loss_ref[...] = loss_in[...]
    grad_ref[...] = grad_in[...]


def per_device(n_head, n_vocab, hidden_states, head_weight, tags, targets, row_grad):
    local, depth = hidden_states.shape
    columns = head_weight.shape[2]
    own = n_head * CAP
    n_chip = n_vocab // 2
    group = n_vocab * own
    chunks = CHUNKS
    vmem = pl.BlockSpec(memory_space=pltpu.VMEM)
    dma = pltpu.SemaphoreType.DMA
    loss, grad = pl.pallas_call(
        functools.partial(kernel, n_head, n_vocab, chunks, BATCHES),
        out_shape=(
            jax.ShapeDtypeStruct((1, local), BF16),
            jax.ShapeDtypeStruct((local, depth), BF16),
        ),
        in_specs=[vmem, vmem, vmem, vmem, pl.BlockSpec(memory_space=pl.ANY)],
        out_specs=(vmem, vmem),
        scratch_shapes=[
            pltpu.VMEM((depth, columns), BF16),
            pltpu.VMEM((own, depth), F32),
            pltpu.VMEM((n_head, CAP, depth), BF16),
            pltpu.VMEM((n_head, CAP, depth), BF16),
            pltpu.VMEM((n_vocab, own, depth), BF16),
            pltpu.VMEM((n_head, own, 128), F32),
            pltpu.VMEM((n_head, own, 128), F32),
            pltpu.VMEM((n_vocab, own, 128), F32),
            pltpu.VMEM((group, columns), F32),
            pltpu.VMEM((group, columns), BF16),
            pltpu.VMEM((n_vocab, 8, group), F32),
            pltpu.VMEM((2, 2, n_chip, own, depth // BATCHES), F32),
            pltpu.VMEM((n_chip, own, depth), BF16),
            pltpu.VMEM((n_chip, own, depth), BF16),
            pltpu.VMEM((n_chip, own, depth), BF16),
            pltpu.VMEM((n_chip, own, depth), BF16),
            pltpu.VMEM((n_head, CAP, depth), BF16),
            pltpu.VMEM((n_head, CAP, depth), BF16),
            pltpu.VMEM((own, 128), F32),
            pltpu.VMEM((n_head, own, 128), F32),
            dma((chunks,)),
            dma, dma((BATCHES,)),
            dma, dma,
            dma, dma((BATCHES,)),
            dma, dma((BATCHES,)),
            dma, dma,
            dma, dma,
            dma, dma((BATCHES,)),
            dma, dma((BATCHES,)),
            dma, dma((BATCHES,)),
            dma, dma,
        ],
        compiler_params=pltpu.CompilerParams(
            collective_id=0, has_side_effects=True, vmem_limit_bytes=56 * 1024 * 1024
        ),
    )(tags.reshape(1, local), targets.reshape(1, local), row_grad.reshape(1, local), hidden_states, head_weight)
    loss, grad = pl.pallas_call(
        hand_over,
        out_shape=(
            jax.ShapeDtypeStruct((1, local), BF16),
            jax.ShapeDtypeStruct((local, depth), BF16),
        ),
        in_specs=[vmem, vmem],
        out_specs=(vmem, vmem),
    )(loss, grad)
    return loss.reshape(local), grad


def solution(mesh):
    placed = (
        P(("head", "vocab"), None),
        P("head", None, "vocab"),
        P(("head", "vocab"), None),
        P(("head", "vocab")),
        P(("head", "vocab")),
    )
    return jax.shard_map(
        functools.partial(per_device, mesh.shape["head"], mesh.shape["vocab"]),
        mesh=mesh,
        in_specs=placed,
        out_specs=(P(("head", "vocab")), P(("head", "vocab"), None)),
        check_vma=False,
    )
```
